512 devices in a mesh: row: 4 (over x), col: 64 (over z, y), leaf: 2 (over core).
Axes of the slice: x: 4, y: 8, z: 8, core: 2. Of those that a mesh axis runs over, the one named last changes fastest.
Arguments:
- bottom_rhs: bfloat16 [512, 256, 128], P(('row', 'col', 'leaf')), may hold values from -6 to 6
- top_rhs: bfloat16 [8, 256, 128], P('row'), may hold values from -6 to 6
- bottom_linv: bfloat16 [512, 256, 256], P(('row', 'col', 'leaf')), may hold values from -2 to 2
- bottom_uinv: bfloat16 [512, 256, 256], P(('row', 'col', 'leaf')), may hold values from -2 to 2
- top_linv: bfloat16 [8, 256, 256], P('row'), may hold values from -2 to 2
- top_uinv: bfloat16 [8, 256, 256], P('row'), may hold values from -2 to 2
- lower_blocks: bfloat16 [8, 64, 2, 4, 256, 256], P('row', 'col', 'leaf'), may hold values from -0.0234375 to 0.0234375
- upper_blocks: bfloat16 [8, 64, 2, 4, 256, 256], P('row', 'col', 'leaf'), may hold values from -0.1875 to 0.1875
- bottom_width: int32 [512], P(('row', 'col', 'leaf')), may hold values from 128 to 256
- top_width: int32 [8], P('row'), may hold values from 128 to 256
- pattern: int32 [8, 64, 2, 4], P('row', 'col', 'leaf'), may hold values 0 or 1
- parent: int32 [64, 2, 4], P('col', 'leaf'), may hold values from 0 to 7
Outputs:
- bottom_solution: float32 [512, 256, 128], P(('row', 'col', 'leaf'))
- top_solution: float32 [8, 256, 128], P('row')
The draws below stay inside these ranges and needn't reach their ends.
All inputs are finite; a program needn't handle non-finite values. No bound on the sum of `pattern` on one device may be relied on, other than what follows from the above.
Results may differ from the reference program's by a relative error of at most 0.0056.
Values may be sent and summed in bfloat16 or wider, within the bound.
A program may use at most 64 MiB of HBM per device.

```python
import jax
import jax.numpy as jnp
from jax import lax

W = 256
NRHS = 128
BD = 1
ST = 8
NCB = 4
NBOT = 512
N_ROW = 4
N_COL = 64
N_LEAF = 2


def assemble(diagonal, offdiag, lower):
    rows = jnp.arange(W, dtype=jnp.int32)[:, None]
    cols = jnp.arange(W, dtype=jnp.int32)[None, :]
    if lower:
        strict = (rows > cols).astype(jnp.float32)
    else:
        strict = (rows < cols).astype(jnp.float32)
    identity = (rows == cols).astype(jnp.float32)
    return offdiag * strict[None] + diagonal[..., None] * identity[None]


def pieces(key, count):
    first, second = jax.random.split(key)
    diagonal = jnp.exp(jax.random.uniform(first, (count, W), jnp.float32, jnp.log(0.5), jnp.log(2.0)))
    offdiag = jnp.clip(jax.random.normal(second, (count, W, W), jnp.float32), -4.0, 4.0) * 0.6 / W ** 0.5
    return (diagonal, offdiag)


def draw_bottom_linv(key, part):
    key = jax.random.fold_in(key, 11)
    diagonal, offdiag = pieces(key, NBOT)
    return assemble(diagonal, offdiag, True).astype(jnp.bfloat16)


def draw_bottom_uinv(key, part):
    key = jax.random.fold_in(key, 12)
    diagonal, offdiag = pieces(key, NBOT)
    return assemble(diagonal, offdiag, False).astype(jnp.bfloat16)


def draw_top_linv(key, part):
    key = jax.random.fold_in(key, 13)
    diagonal, offdiag = pieces(key, ST)
    return assemble(diagonal, offdiag, True).astype(jnp.bfloat16)


def draw_top_uinv(key, part):
    key = jax.random.fold_in(key, 14)
    diagonal, offdiag = pieces(key, ST)
    return assemble(diagonal, offdiag, False).astype(jnp.bfloat16)


def touch_ends(entries, key, smallest, high):
    dims = entries.shape
    spot = [jax.random.randint(jax.random.fold_in(key, axis), (), 0, dims[axis]) for axis in range(len(dims))]
    entries = entries.at[tuple(spot)].set(smallest)
    longest = dims.index(max(dims))
    spot[longest] = (spot[longest] + 1) % dims[longest]
    return entries.at[tuple(spot)].set(high)


def levels(key, extent, cuts, smallest, high):
    gain, own = 1.0, jax.random.fold_in(key, 6)
    for dim, blocks in cuts:
        heights = jnp.exp(jax.random.uniform(jax.random.fold_in(own, dim), (blocks,), jnp.float32, smallest / len(cuts), high / len(cuts)))
        gain = gain * jnp.repeat(heights, extent[dim] // blocks).reshape([-1 if axis == dim else 1 for axis in range(len(extent))])
    return gain


def centred(own_key, dims, width, limit, cuts=(), held_as=jnp.bfloat16):
    array = width * jax.random.normal(own_key, dims, jnp.float32)
    if cuts:
        array = array * levels(own_key, dims, cuts, -0.22, 0.18)
    return jnp.clip(array, -limit, limit).astype(held_as)


def setup_inputs(seed: int = 0) -> dict:
    streams_of = jax.random.split(jax.random.key(seed), 13)
    return {
        "bottom_rhs": centred(streams_of[0], (NBOT, W, NRHS), 1.0, 6.0, ((0, 512),)),
        "top_rhs": centred(streams_of[1], (ST, W, NRHS), 1.0, 6.0, ((0, 4),)),
        "bottom_linv": draw_bottom_linv(jax.random.fold_in(streams_of[12], 71), 0),
        "bottom_uinv": draw_bottom_uinv(jax.random.fold_in(streams_of[12], 71), 0),
        "top_linv": draw_top_linv(jax.random.fold_in(streams_of[12], 71), 0),
        "top_uinv": draw_top_uinv(jax.random.fold_in(streams_of[12], 71), 0),
        "lower_blocks": centred(streams_of[6], (ST, N_COL, N_LEAF, NCB, W, W), (W * N_COL * N_LEAF * NCB // 2) ** -0.5, 0.0234375, ((0, 4), (1, 64), (2, 2))),
        "upper_blocks": centred(streams_of[7], (ST, N_COL, N_LEAF, NCB, W, W), (W * ST // 2) ** -0.5, 0.1875, ((0, 4), (1, 64), (2, 2))),
        "bottom_width": touch_ends(jax.random.randint(streams_of[8], (NBOT,), W // 2, W + 1), jax.random.fold_in(streams_of[8], 1), W // 2, W).astype(jnp.int32),
        "top_width": touch_ends(jax.random.randint(streams_of[9], (ST,), W // 2, W + 1), jax.random.fold_in(streams_of[9], 1), W // 2, W).astype(jnp.int32),
        "pattern": touch_ends((jax.random.randint(streams_of[10], (ST, N_COL, N_LEAF, NCB), 0, 2) < 1).astype(jnp.int32), jax.random.fold_in(streams_of[10], 1), 0, 1),
        "parent": touch_ends(jax.random.randint(streams_of[11], (N_COL, N_LEAF, NCB), 0, ST), jax.random.fold_in(streams_of[11], 1), 0, ST - 1).astype(jnp.int32),
    }


def apply_blocks(blocks, vectors):
    return jnp.einsum("bvw,bwn->bvn", blocks.astype(jnp.float32), vectors.astype(jnp.float32), precision=lax.Precision.HIGHEST)


def reference(bottom_rhs, top_rhs, bottom_linv, bottom_uinv, top_linv, top_uinv, lower_blocks, upper_blocks, bottom_width, top_width, pattern, parent):
    places = jnp.arange(W, dtype=jnp.int32)
    bottom_mask = (places[None, :] < bottom_width[:, None]).astype(jnp.float32)
    top_mask = (places[None, :] < top_width[:, None]).astype(jnp.float32)
    tops = jnp.arange(ST, dtype=jnp.int32)
    couple = ((pattern > 0) | (parent[None] == tops[:, None, None, None])).astype(jnp.bfloat16)
    masked_rhs = bottom_rhs * bottom_mask.astype(jnp.bfloat16)[..., None]
    bottom_y = (apply_blocks(bottom_linv, masked_rhs) * bottom_mask[..., None]).astype(jnp.bfloat16)
    column_values = bottom_y.reshape(N_ROW, N_COL, N_LEAF, BD, W, NRHS)
    column_values = jnp.transpose(column_values, (1, 2, 0, 3, 4, 5)).reshape(N_COL, N_LEAF, NCB, W, NRHS)

    def forward_step(column, total):
        blocks = lax.dynamic_index_in_dim(lower_blocks, column, 1, keepdims=False)
        weights = lax.dynamic_index_in_dim(couple, column, 1, keepdims=False)
        values = lax.dynamic_index_in_dim(column_values, column, 0, keepdims=False)
        masked = (blocks * weights[..., None, None]).astype(jnp.float32)
        return total + jnp.einsum("tljvw,ljwn->tvn", masked, values.astype(jnp.float32), precision=lax.Precision.HIGHEST)

    lsum = lax.fori_loop(0, N_COL, forward_step, jnp.zeros((ST, W, NRHS), jnp.float32))
    top_diff = ((top_rhs.astype(jnp.float32) - lsum) * top_mask[..., None]).astype(jnp.bfloat16)
    top_y = (apply_blocks(top_linv, top_diff) * top_mask[..., None]).astype(jnp.bfloat16)
    top_solution = apply_blocks(top_uinv, top_y) * top_mask[..., None]
    top_half = top_solution.astype(jnp.bfloat16)

    def backward_column(column):
        blocks = lax.dynamic_index_in_dim(upper_blocks, column, 1, keepdims=False)
        weights = lax.dynamic_index_in_dim(couple, column, 1, keepdims=False)
        masked = (blocks * weights[..., None, None]).astype(jnp.float32)
        return jnp.einsum("tljvw,twn->ljvn", masked, top_half.astype(jnp.float32), precision=lax.Precision.HIGHEST)

    usum = lax.map(backward_column, jnp.arange(N_COL, dtype=jnp.int32))
    usum = usum.reshape(N_COL, N_LEAF, N_ROW, BD, W, NRHS)
    usum = jnp.transpose(usum, (2, 0, 1, 3, 4, 5)).reshape(NBOT, W, NRHS)
    bottom_diff = ((bottom_y.astype(jnp.float32) - usum) * bottom_mask[..., None]).astype(jnp.bfloat16)
    bottom_solution = apply_blocks(bottom_uinv, bottom_diff) * bottom_mask[..., None]
    return bottom_solution, top_solution
```

```python
import functools

import jax
import jax.numpy as jnp
from jax import lax
from jax.experimental import pallas as pl
from jax.experimental.pallas import tpu as pltpu
from jax.sharding import PartitionSpec as P

MESH = pl.DeviceIdType.MESH
F32 = jnp.float32
BF16 = jnp.bfloat16

W = 256
NRHS = 128
TPR = 2
NCB = 4
SIDE = 8
CHUNKS = 8
CH = TPR * W // CHUNKS

NEAR = ((0, 0), (0, 1), (-1, 0), (-1, 1), (-2, 0), (1, -1), (1, 0), (0, -1))
NEAR_ORDER = (4, 3, 5, 1, 2, 6, 7, 0)
FAR_ORDER = (2, 6, 3, 5, 4, 1, 7)
X_ORDER = (2, 1, 3)


def kernel(
    brhs_h,
    trhs_h,
    blinv_h,
    buinv_h,
    tlinv_h,
    tuinv_h,
    low_h,
    up_h,
    bw_ref,
    tw_ref,
    pat_ref,
    par_ref,
    bsol_ref,
    tsol_ref,
    brhs,
    trhs,
    blinv,
    buinv,
    tlinv,
    tuinv,
    low,
    up,
    ybuf,
    acc,
    part,
    rsbuf,
    midbuf,
    diff,
    ucon,
    ubuf,
    in_sem,
    xs_sem,
    xr_sem,
    rs_s,
    rs_r,
    mid_s,
    mid_r,
    ag_s,
    ag_r,
    us_s,
    us_r,
):
    row = lax.axis_index("row")
    col = lax.axis_index("col")
    leaf = lax.axis_index("leaf")
    z, y = lax.div(col, SIDE), lax.rem(col, SIDE)
    kind = lax.rem(y - 2 * z + 2 * SIDE, SIDE)

    def at(dz, dy, to_leaf):
        zz = lax.rem(z + (dz + SIDE), SIDE)
        yy = lax.rem(y + (dy + 2 * SIDE), SIDE)
        return (row, zz * SIDE + yy, to_leaf)

    def along(dx):
        return (lax.rem(row + dx, NCB), col, leaf)

    loads = []
    for i, (src, dst) in enumerate(
        (
            (blinv_h.at[0], blinv),
            (brhs_h.at[0], brhs),
            (low_h.at[:, 0, 0], low),
            (trhs_h, trhs),
            (tlinv_h, tlinv),
            (tuinv_h, tuinv),
            (up_h.at[:, 0, 0], up),
            (buinv_h.at[0], buinv),
        )
    ):
        load = pltpu.make_async_copy(src, dst, in_sem.at[i])
        load.start()
        loads.append(load)
    ld_blinv, ld_brhs, ld_low, ld_trhs, ld_tlinv, ld_tuinv, ld_up, ld_buinv = loads

    def hello(device):
        pl.semaphore_signal(barrier, inc=1, device_id=device, device_id_type=MESH)

    barrier = pltpu.get_barrier_semaphore()
    for dx in (1, 2, 3):
        hello(along(dx))
    for dz, dy in NEAR[1:]:
        hello(at(dz, dy, 1))

    @pl.when(leaf == 0)
    def _():
        hello(at(0, 0, 1))

    @pl.when(leaf == 1)
    def _():
        for dz, dy in NEAR:
            hello(at(-dz, -dy, 0))
        hello(at(2, 0, 1))
        for i in range(1, SIDE):
            hello(at(i, 2 * i, 1))

    places = lax.broadcasted_iota(jnp.int32, (W, NRHS), 0)
    bmask = places < bw_ref[0]

    def masked(value, mask):
        return jnp.where(mask, value, jnp.zeros_like(value))

    def dot(a, b):
        return jnp.dot(a, b, preferred_element_type=F32)

    ld_brhs.wait()
    ld_blinv.wait()
    rhs = masked(brhs[...].astype(F32), bmask).astype(BF16)
    own_y = masked(dot(blinv[...], rhs), bmask).astype(BF16)
    ybuf[row] = own_y

    pl.semaphore_wait(barrier, jnp.where(leaf == 1, 26, 11))

    xsends = []
    for dx in X_ORDER:
        send = pltpu.make_async_remote_copy(
            src_ref=ybuf.at[row],
            dst_ref=ybuf.at[row],
            send_sem=xs_sem.at[dx],
            recv_sem=xr_sem.at[dx],
            device_id=along(dx),
            device_id_type=MESH,
        )
        send.start()
        xsends.append(send)

    def couple(t, j):
        on = (pat_ref[t, 0, 0, j] > 0) | (par_ref[0, 0, j] == row * TPR + t)
        return jnp.where(on, 1.0, 0.0).astype(F32)

    def arrived(sem, dx, ref):
        pltpu.make_async_remote_copy(
            src_ref=ref,
            dst_ref=ref,
            send_sem=xs_sem.at[0],
            recv_sem=sem.at[dx],
            device_id=along(dx),
            device_id_type=MESH,
        ).wait_recv()

    ld_low.wait()
    for step, back in enumerate((0, 1, 3, 2)):
        j = lax.rem(row + NCB - back, NCB)
        if back:
            arrived(xr_sem, back, ybuf.at[j])
        vec = ybuf[j]
        for t in range(TPR):
            term = dot(low[t, j], vec) * couple(t, j)
            rows = pl.ds(t * W, W)
            if step == 0:
                acc[rows, :] = term
            elif step < NCB - 1:
                acc[rows, :] += term
            else:
                total = acc[rows, :] + term
                acc[rows, :] = total
                part[rows, :] = total.astype(BF16)

    def chunk(k):
        return pl.ds(pl.multiple_of(k * CH, CH), CH)

    def near_copy(m, to_leaf, slot):
        dz, dy = NEAR[m]
        k = lax.rem(kind + m, CHUNKS)
        return pltpu.make_async_remote_copy(
            src_ref=part.at[chunk(k)],
            dst_ref=rsbuf.at[slot],
            send_sem=rs_s.at[m],
            recv_sem=rs_r.at[slot],
            device_id=at(dz, dy, to_leaf),
            device_id_type=MESH,
        )

    @pl.when(leaf == 0)
    def _():
        for m in NEAR_ORDER:
            near_copy(m, 1, CHUNKS + m).start()

    own = chunk(kind)

    def back_copy(m, to_leaf):
        dz, dy = NEAR[m]
        return pltpu.make_async_remote_copy(
            src_ref=diff.at[own],
            dst_ref=diff.at[own],
            send_sem=ag_s.at[to_leaf, m],
            recv_sem=ag_r.at[m],
            device_id=at(-dz, -dy, to_leaf),
            device_id_type=MESH,
        )

    @pl.when(leaf == 1)
    def _():
        for m in NEAR_ORDER:
            if m:
                near_copy(m, 1, m).start()
        total = acc[own, :]
        for m in NEAR_ORDER:
            if m:
                near_copy(m, 1, m).wait_recv()
                total += rsbuf[m].astype(F32)
        for m in NEAR_ORDER:
            near_copy(m, 1, CHUNKS + m).wait_recv()
            total += rsbuf[CHUNKS + m].astype(F32)
        midbuf[z] = total.astype(BF16)

        fars = []
        for i in FAR_ORDER:
            far = pltpu.make_async_remote_copy(
                src_ref=midbuf.at[z],
                dst_ref=midbuf.at[z],
                send_sem=mid_s.at[i],
                recv_sem=mid_r.at[i],
                device_id=at(i, 2 * i, 1),
                device_id_type=MESH,
            )
            far.start()
            fars.append(far)
        ld_trhs.wait()
        for far in fars:
            far.wait_recv()
        lsum = midbuf[0].astype(F32)
        for i in range(1, SIDE):
            lsum += midbuf[i].astype(F32)
        top = lax.div(kind, CHUNKS // TPR)
        first = lax.rem(kind, CHUNKS // TPR) * CH
        here = lax.broadcasted_iota(jnp.int32, (CH, NRHS), 0) + first
        rest = trhs[top, pl.ds(pl.multiple_of(first, CH), CH), :].astype(F32) - lsum
        diff[own, :] = masked(rest, here < tw_ref[top]).astype(BF16)
        for to_leaf in (0, 1):
            for m in NEAR_ORDER:
                if m or to_leaf == 0:
                    back_copy(m, to_leaf).start()
        for far in fars:
            far.wait_send()
        for m in NEAR_ORDER:
            if m:
                near_copy(m, 1, m).wait_send()

    @pl.when(leaf == 0)
    def _():
        ld_trhs.wait()
        for m in NEAR_ORDER:
            near_copy(m, 1, CHUNKS + m).wait_send()
        back_copy(0, 0).wait_recv()

    for m in NEAR_ORDER:
        if m:
            back_copy(m, 0).wait_recv()

    ld_tlinv.wait()
    ld_tuinv.wait()
    halves = []
    for t in range(TPR):
        tmask = places < tw_ref[t]
        top_y = masked(dot(tlinv[t], diff[pl.ds(t * W, W), :]), tmask).astype(BF16)
        top = masked(dot(tuinv[t], top_y), tmask)
        tsol_ref[t] = top
        halves.append(top.astype(BF16))

    ld_up.wait()
    usends = []
    mine = None
    for dx in X_ORDER + (0,):
        j = lax.rem(row + dx, NCB)
        term = dot(up[0, j], halves[0]) * couple(0, j)
        term += dot(up[1, j], halves[1]) * couple(1, j)
        if dx == 0:
            mine = term
            break
        ucon[dx] = term.astype(BF16)
        send = pltpu.make_async_remote_copy(
            src_ref=ucon.at[dx],
            dst_ref=ubuf.at[dx],
            send_sem=us_s.at[dx],
            recv_sem=us_r.at[dx],
            device_id=along(dx),
            device_id_type=MESH,
        )
        send.start()
        usends.append(send)
    ld_buinv.wait()
    usum = mine
    for send, dx in zip(usends[1:] + usends[:1], (1, 3, 2)):
        send.wait_recv()
        usum += ubuf[dx].astype(F32)
    bdiff = masked(ybuf[row].astype(F32) - usum, bmask).astype(BF16)
    bsol_ref[0] = masked(dot(buinv[...], bdiff), bmask)

    for send in xsends + usends:
        send.wait_send()

    @pl.when(leaf == 1)
    def _():
        for to_leaf in (0, 1):
            for m in NEAR_ORDER:
                if m or to_leaf == 0:
                    back_copy(m, to_leaf).wait_send()


def local(*args):
    hbm = pl.BlockSpec(memory_space=pltpu.HBM)
    smem = pl.BlockSpec(memory_space=pltpu.SMEM)
    vmem = pl.BlockSpec(memory_space=pltpu.VMEM)
    dma = pltpu.SemaphoreType.DMA
    return pl.pallas_call(
        kernel,
        out_shape=(
            jax.ShapeDtypeStruct((1, W, NRHS), F32),
            jax.ShapeDtypeStruct((TPR, W, NRHS), F32),
        ),
        in_specs=[hbm] * 8 + [smem] * 4,
        out_specs=(vmem, vmem),
        scratch_shapes=[
            pltpu.VMEM((W, NRHS), BF16),
            pltpu.VMEM((TPR, W, NRHS), BF16),
            pltpu.VMEM((W, W), BF16),
            pltpu.VMEM((W, W), BF16),
            pltpu.VMEM((TPR, W, W), BF16),
            pltpu.VMEM((TPR, W, W), BF16),
            pltpu.VMEM((TPR, NCB, W, W), BF16),
            pltpu.VMEM((TPR, NCB, W, W), BF16),
            pltpu.VMEM((NCB, W, NRHS), BF16),
            pltpu.VMEM((TPR * W, NRHS), F32),
            pltpu.VMEM((TPR * W, NRHS), BF16),
            pltpu.VMEM((2 * CHUNKS, CH, NRHS), BF16),
            pltpu.VMEM((SIDE, CH, NRHS), BF16),
            pltpu.VMEM((TPR * W, NRHS), BF16),
            pltpu.VMEM((NCB, W, NRHS), BF16),
            pltpu.VMEM((NCB, W, NRHS), BF16),
            dma((8,)),
            dma((NCB,)),
            dma((NCB,)),
            dma((CHUNKS,)),
            dma((2 * CHUNKS,)),
            dma((SIDE,)),
            dma((SIDE,)),
            dma((2, CHUNKS)),
            dma((CHUNKS,)),
            dma((NCB,)),
            dma((NCB,)),
        ],
        compiler_params=pltpu.CompilerParams(
            collective_id=0, has_side_effects=True, vmem_limit_bytes=32 << 20
        ),
        name="substitution",
    )(*args)


def solution(mesh):
    placed = (
        P(("row", "col", "leaf"), None, None),
        P("row", None, None),
        P(("row", "col", "leaf"), None, None),
        P(("row", "col", "leaf"), None, None),
        P("row", None, None),
        P("row", None, None),
        P("row", "col", "leaf", None, None, None),
        P("row", "col", "leaf", None, None, None),
        P(("row", "col", "leaf")),
        P("row"),
        P("row", "col", "leaf", None),
        P("col", "leaf", None),
    )
    return jax.shard_map(
        local,
        mesh=mesh,
        in_specs=placed,
        out_specs=(P(("row", "col", "leaf"), None, None), P("row", None, None)),
        check_vma=False,
    )
```

```python
import jax
import jax.numpy as jnp
from jax import lax
from jax.experimental import pallas as pl
from jax.experimental.pallas import tpu as pltpu
from jax.sharding import PartitionSpec as P

MESH = pl.DeviceIdType.MESH
F32 = jnp.float32
BF16 = jnp.bfloat16

W = 256
NRHS = 128
TPR = 2
NCB = 4
SIDE = 8
PLANE = SIDE * SIDE
HUBS = SIDE
CH = TPR * W // HUBS

HUB_ORDER = (4, 3, 5, 2, 6, 1, 7, 0)
NEAR_FIRST = (0, 1, 7, 2, 6, 3, 5, 4)
ROWS = (1, 3, 0, 2)
LATE = 2


def kernel(
    brhs_h,
    trhs_h,
    blinv_h,
    buinv_h,
    tlinv_h,
    tuinv_h,
    low_h,
    up_h,
    bw_h,
    tw_h,
    pat_h,
    par_h,
    bsol_ref,
    tsol_ref,
    brhs,
    trhs,
    blinv,
    buinv,
    tlinv,
    tuinv,
    low,
    up,
    ybuf,
    acc,
    part,
    hubbuf,
    diff,
    ucon,
    ubuf,
    mine,
    cpl,
    bw_ref,
    tw_ref,
    pat_ref,
    par_ref,
    in_sem,
    pair_s,
    pair_r,
    xs_sem,
    xr_sem,
    hub_s,
    hub_r,
    out_s,
    out_r,
    us_s,
    us_r,
    late_sem,
):
    row = lax.axis_index("row")
    col = lax.axis_index("col")
    leaf = lax.axis_index("leaf")
    z, y = lax.div(col, SIDE), lax.rem(col, SIDE)
    late = row == LATE
    is_hub = z == 0

    def remote(src, dst, send_sem, recv_sem, device):
        return pltpu.make_async_remote_copy(
            src_ref=src,
            dst_ref=dst,
            send_sem=send_sem,
            recv_sem=recv_sem,
            device_id=device,
            device_id_type=MESH,
        )

    def load(i, src, dst):
        copy = pltpu.make_async_copy(src, dst, in_sem.at[i])
        copy.start()
        return copy

    barrier = pltpu.get_barrier_semaphore()

    def hello(device):
        pl.semaphore_signal(barrier, inc=1, device_id=device, device_id_type=MESH)

    def masked(value, mask):
        return jnp.where(mask, value, jnp.zeros_like(value))

    def dot(a, b):
        return jnp.dot(a, b, preferred_element_type=F32)

    places = lax.broadcasted_iota(jnp.int32, (W, NRHS), 0)

    def along(dx, to_leaf):
        return (lax.rem(row + dx, NCB), col, to_leaf)

    def own_y(ld_bw, ld_brhs, ld_blinv):
        ld_bw.wait()
        ld_brhs.wait()
        ld_blinv.wait()
        bmask = places < bw_ref[0]
        rhs = masked(brhs[...].astype(F32), bmask).astype(BF16)
        return bmask, masked(dot(blinv[...], rhs), bmask).astype(BF16)

    def couples(layer, ld_pat, ld_par):
        ld_pat.wait()
        ld_par.wait()
        for t in range(TPR):
            for j in range(NCB):
                on = (pat_ref[t, 0, 0, j] > 0) | (par_ref[0, 0, j] == row * TPR + t)
                cpl[layer, pl.ds(t * NCB + j, 1), :] = jnp.full(
                    (1, NRHS), jnp.where(on, 1.0, 0.0), F32
                )

    def finish(layer, bmask, own, ld_buinv):
        usum = jnp.zeros((W, NRHS), F32)
        for s in ROWS:

            @pl.when(s != row)
            def _():
                remote(
                    ubuf.at[s], ubuf.at[s], us_s.at[0, 0], us_r.at[s], along(1, layer)
                ).wait_recv()

            usum += jnp.where(s == row, own, ubuf[s].astype(F32))
        ld_buinv.wait()
        bdiff = masked(ybuf[layer, row].astype(F32) - usum, bmask).astype(BF16)
        bsol_ref[0] = masked(dot(buinv[...], bdiff), bmask)

    @pl.when(leaf == 0)
    def _():
        pair = (row, col, 1)
        ld_blinv = load(0, blinv_h.at[0], blinv)
        ld_brhs = load(1, brhs_h.at[0], brhs)
        ld_bw = load(2, bw_h, bw_ref)
        ld_pat = load(3, pat_h, pat_ref)
        ld_par = load(4, par_h, par_ref)
        ld_buinv = load(5, buinv_h.at[0], buinv)
        bmask, value = own_y(ld_bw, ld_brhs, ld_blinv)
        ybuf[0, row] = value
        couples(0, ld_pat, ld_par)
        pl.semaphore_wait(barrier, 1)
        sends = [
            remote(ybuf.at[0, row], ybuf.at[0, row], pair_s.at[0], pair_r.at[0], pair),
            remote(cpl.at[0], cpl.at[0], pair_s.at[1], pair_r.at[1], pair),
            remote(low_h.at[:, 0, 0], low.at[0], pair_s.at[2], pair_r.at[2], pair),
            remote(up_h.at[:, 0, 0], up.at[0], pair_s.at[3], pair_r.at[3], pair),
        ]
        for send in sends:
            send.start()
        for send in sends:
            send.wait_send()
        remote(mine, mine, pair_s.at[4], pair_r.at[4], pair).wait_recv()
        finish(0, bmask, mine[...], ld_buinv)
        remote(tsol_ref, tsol_ref, pair_s.at[5], pair_r.at[5], pair).wait_recv()

    def to_hub(h):
        rows = pl.ds(h * CH, CH)
        return remote(
            part.at[rows], hubbuf.at[col], hub_s.at[h], hub_r.at[col], (row, h, 1)
        )

    def hand(k, to_z, to_y):
        rows = pl.ds(pl.multiple_of(k * CH, CH), CH)
        return remote(
            diff.at[rows],
            diff.at[rows],
            out_s.at[lax.rem(z + SIDE - to_z, SIDE) if to_z is not z else SIDE + to_y],
            out_r.at[k],
            (row, to_z * SIDE + to_y, 1),
        )

    @pl.when(leaf == 1)
    def _():
        pair = (row, col, 0)
        ld_blinv = load(0, blinv_h.at[0], blinv)
        ld_brhs = load(1, brhs_h.at[0], brhs)
        ld_bw = load(2, bw_h, bw_ref)
        hello(pair)

        @pl.when(jnp.logical_not(late))
        def _():
            for dx in (2, 1, 3):
                hello(along(dx, 1))

        ld_pat = load(3, pat_h, pat_ref)
        ld_par = load(4, par_h, par_ref)
        ld_low = load(6, low_h.at[:, 0, 0], low.at[1])
        ld_tw = load(7, tw_h, tw_ref)
        ld_trhs = load(8, trhs_h, trhs)
        ld_tlinv = load(9, tlinv_h, tlinv)
        ld_tuinv = load(10, tuinv_h, tuinv)
        ld_up = load(11, up_h.at[:, 0, 0], up.at[1])
        ld_buinv = load(5, buinv_h.at[0], buinv)

        @pl.when(is_hub)
        def _():
            def greet(c, carry):
                @pl.when(c != col)
                def _():
                    hello((row, c, 1))

                return carry

            lax.fori_loop(0, PLANE, greet, 0)

        hubs = jnp.where(is_hub, HUBS - 1, HUBS)

        @pl.when(late)
        def _():
            pl.semaphore_wait(barrier, hubs + NCB - 1)
            for dx in (2, 1, 3):
                pl.semaphore_signal(
                    late_sem, inc=1, device_id=along(dx, 1), device_id_type=MESH
                )

        bmask, value = own_y(ld_bw, ld_brhs, ld_blinv)
        ybuf[1, row] = value

        @pl.when(jnp.logical_not(late))
        def _():
            pl.semaphore_wait(barrier, hubs + NCB - 2)

        def send_y(layer, to):
            return remote(
                ybuf.at[layer, row],
                ybuf.at[layer, row],
                xs_sem.at[layer, to],
                xr_sem.at[layer, row],
                (to, col, 1),
            )

        def wait_y0():
            remote(
                ybuf.at[0, row], ybuf.at[0, row], pair_s.at[0], pair_r.at[0], pair
            ).wait_recv()

        for layer in (1, 0):
            if layer == 0:
                wait_y0()
            for dx in (2, 1, 3):
                to = lax.rem(row + dx, NCB)

                @pl.when(late | (to != LATE))
                def _():
                    send_y(layer, to).start()

        @pl.when(jnp.logical_not(late))
        def _():
            pl.semaphore_wait(late_sem, 1)
            for layer in (1, 0):
                send_y(layer, LATE).start()

        couples(1, ld_pat, ld_par)
        ld_low.wait()
        remote(cpl.at[0], cpl.at[0], pair_s.at[1], pair_r.at[1], pair).wait_recv()
        remote(
            low_h.at[:, 0, 0], low.at[0], pair_s.at[2], pair_r.at[2], pair
        ).wait_recv()

        def factor(layer, t, j):
            return cpl[layer, pl.ds(t * NCB + j, 1), :]

        order = (
            row,
            jnp.where(lax.rem(row, 2) == 0, 1, 0),
            jnp.where(row == NCB - 1, 1, NCB - 1),
            jnp.where(late, 0, LATE),
        )
        steps = [(layer, i) for i in range(NCB) for layer in (1, 0)]
        for step, (layer, i) in enumerate(steps):
            s = order[i]
            if i:
                remote(
                    ybuf.at[layer, s],
                    ybuf.at[layer, s],
                    xs_sem.at[layer, s],
                    xr_sem.at[layer, s],
                    (s, col, 1),
                ).wait_recv()
            vec = ybuf[layer, s]
            if step < len(steps) - 1:
                for t in range(TPR):
                    term = dot(low[layer, t, s], vec) * factor(layer, t, s)
                    rows = pl.ds(t * W, W)
                    if step == 0:
                        acc[rows, :] = term
                    else:
                        acc[rows, :] += term
                continue
            for h in HUB_ORDER:
                t, first = h // (HUBS // TPR), h % (HUBS // TPR) * CH
                term = dot(low[layer, t, s, pl.ds(first, CH), :], vec)
                term *= factor(layer, t, s)
                rows = pl.ds(h * CH, CH)
                part[rows, :] = (acc[rows, :] + term).astype(BF16)

                @pl.when(col != h)
                def _():
                    to_hub(h).start()

        @pl.when(is_hub)
        def _():
            own = pl.ds(pl.multiple_of(y * CH, CH), CH)
            hubbuf[col] = part[own, :]

            def add(c, total):
                @pl.when(c != col)
                def _():
                    remote(
                        part.at[own], hubbuf.at[c], hub_s.at[0], hub_r.at[c], (row, c, 1)
                    ).wait_recv()

                return total + hubbuf[c].astype(F32)

            lsum = lax.fori_loop(0, PLANE, add, jnp.zeros((CH, NRHS), F32))
            ld_tw.wait()
            ld_trhs.wait()
            top = lax.div(y, HUBS // TPR)
            first = lax.rem(y, HUBS // TPR) * CH
            here = lax.broadcasted_iota(jnp.int32, (CH, NRHS), 0) + first
            width = jnp.where(top == 0, tw_ref[0], tw_ref[1])
            rest = trhs[top, pl.ds(pl.multiple_of(first, CH), CH), :].astype(F32) - lsum
            diff[own, :] = masked(rest, here < width).astype(BF16)

        @pl.when(jnp.logical_not(is_hub))
        def _():
            ld_tw.wait()
            ld_trhs.wait()
            hand(y, 0, y).wait_recv()

        for to in NEAR_FIRST:

            @pl.when(y != to)
            def _():
                hand(y, z, to).start()

        @pl.when(is_hub)
        def _():
            for to in NEAR_FIRST[1:]:
                hand(y, to, y).start()

        ld_tlinv.wait()
        ld_tuinv.wait()
        halves = []
        for t in range(TPR):
            for k in range(t * HUBS // TPR, (t + 1) * HUBS // TPR):

                @pl.when(y != k)
                def _():
                    hand(k, z, k).wait_recv()

            tmask = places < tw_ref[t]
            top_y = masked(dot(tlinv[t], diff[pl.ds(t * W, W), :]), tmask).astype(BF16)
            top = masked(dot(tuinv[t], top_y), tmask)
            tsol_ref[t] = top
            halves.append(top.astype(BF16))

        ld_up.wait()
        remote(up_h.at[:, 0, 0], up.at[0], pair_s.at[3], pair_r.at[3], pair).wait_recv()

        def contribution(layer, j):
            total = dot(up[layer, 0, j], halves[0]) * factor(layer, 0, j)
            return total + dot(up[layer, 1, j], halves[1]) * factor(layer, 1, j)

        sends = []
        for layer in (1, 0):
            for dx in (2, 1, 3):
                j = lax.rem(row + dx, NCB)
                ucon[layer, dx] = contribution(layer, j).astype(BF16)
                send = remote(
                    ucon.at[layer, dx],
                    ubuf.at[row],
                    us_s.at[layer, dx],
                    us_r.at[row],
                    (j, col, layer),
                )
                send.start()
                sends.append(send)
        mine[...] = contribution(0, row)
        sends.append(remote(mine, mine, pair_s.at[4], pair_r.at[4], pair))
        sends[-1].start()
        sends.append(remote(tsol_ref, tsol_ref, pair_s.at[5], pair_r.at[5], pair))
        sends[-1].start()
        own = contribution(1, row)

        finish(1, bmask, own, ld_buinv)
        for send in sends:
            send.wait_send()
        for layer in (1, 0):
            for dx in (1, 2, 3):
                send_y(layer, lax.rem(row + dx, NCB)).wait_send()
        for h in range(HUBS):

            @pl.when(col != h)
            def _():
                to_hub(h).wait_send()

            @pl.when(y != h)
            def _():
                hand(y, z, h).wait_send()

        @pl.when(is_hub)
        def _():
            for to in NEAR_FIRST[1:]:
                hand(y, to, y).wait_send()


def local(*args):
    hbm = pl.BlockSpec(memory_space=pltpu.HBM)
    vmem = pl.BlockSpec(memory_space=pltpu.VMEM)
    dma = pltpu.SemaphoreType.DMA
    return pl.pallas_call(
        kernel,
        out_shape=(
            pltpu.VMEM((1, W, NRHS), F32),
            pltpu.VMEM((TPR, W, NRHS), F32),
        ),
        in_specs=[hbm] * 12,
        out_specs=(vmem, vmem),
        scratch_shapes=[
            pltpu.VMEM((W, NRHS), BF16),
            pltpu.VMEM((TPR, W, NRHS), BF16),
            pltpu.VMEM((W, W), BF16),
            pltpu.VMEM((W, W), BF16),
            pltpu.VMEM((TPR, W, W), BF16),
            pltpu.VMEM((TPR, W, W), BF16),
            pltpu.VMEM((2, TPR, NCB, W, W), BF16),
            pltpu.VMEM((2, TPR, NCB, W, W), BF16),
            pltpu.VMEM((2, NCB, W, NRHS), BF16),
            pltpu.VMEM((TPR * W, NRHS), F32),
            pltpu.VMEM((TPR * W, NRHS), BF16),
            pltpu.VMEM((PLANE, CH, NRHS), BF16),
            pltpu.VMEM((TPR * W, NRHS), BF16),
            pltpu.VMEM((2, NCB, W, NRHS), BF16),
            pltpu.VMEM((NCB, W, NRHS), BF16),
            pltpu.VMEM((W, NRHS), F32),
            pltpu.VMEM((2, TPR * NCB, NRHS), F32),
            pltpu.SMEM((1,), jnp.int32),
            pltpu.SMEM((TPR,), jnp.int32),
            pltpu.SMEM((TPR, 1, 1, NCB), jnp.int32),
            pltpu.SMEM((1, 1, NCB), jnp.int32),
            dma((12,)),
            dma((6,)),
            dma((6,)),
            dma((2, NCB)),
            dma((2, NCB)),
            dma((HUBS,)),
            dma((PLANE,)),
            dma((2 * SIDE,)),
            dma((HUBS,)),
            dma((2, NCB)),
            dma((NCB,)),
            pltpu.SemaphoreType.REGULAR,
        ],
        compiler_params=pltpu.CompilerParams(
            collective_id=0, has_side_effects=True, vmem_limit_bytes=60 << 20
        ),
        name="substitution",
    )(*args)


def solution(mesh):
    placed = (
        P(("row", "col", "leaf"), None, None),
        P("row", None, None),
        P(("row", "col", "leaf"), None, None),
        P(("row", "col", "leaf"), None, None),
        P("row", None, None),
        P("row", None, None),
        P("row", "col", "leaf", None, None, None),
        P("row", "col", "leaf", None, None, None),
        P(("row", "col", "leaf")),
        P("row"),
        P("row", "col", "leaf", None),
        P("col", "leaf", None),
    )
    return jax.shard_map(
        local,
        mesh=mesh,
        in_specs=placed,
        out_specs=(P(("row", "col", "leaf"), None, None), P("row", None, None)),
        check_vma=False,
    )
```

```python
import jax
import jax.numpy as jnp
from jax import lax
from jax.experimental import pallas as pl
from jax.experimental.pallas import tpu as pltpu
from jax.sharding import PartitionSpec as P

MESH = pl.DeviceIdType.MESH
F32 = jnp.float32
BF16 = jnp.bfloat16

W = 256
NRHS = 128
TPR = 2
NCB = 4
SIDE = 8
PLANE = SIDE * SIDE
HUBS = SIDE
CH = TPR * W // HUBS

HUB_ORDER = (4, 3, 5, 2, 6, 1, 7, 0)
NEAR_FIRST = (0, 1, 7, 2, 6, 3, 5, 4)


def chunk_of(hub):
    if isinstance(hub, int):
        return NEAR_FIRST.index(hub)
    side = jnp.where(hub <= SIDE // 2, 2 * hub - 1, 2 * (SIDE - hub))
    return jnp.where(hub == 0, 0, side)


def chunk_rows(hub):
    first = chunk_of(hub) * CH
    return pl.ds(first if isinstance(first, int) else pl.multiple_of(first, CH), CH)
ROWS = (1, 3, 0, 2)
LATE = 2


def kernel(
    brhs_h,
    trhs_h,
    blinv_h,
    buinv_h,
    tlinv_h,
    tuinv_h,
    low_h,
    up_h,
    bw_h,
    tw_h,
    pat_h,
    par_h,
    bsol_ref,
    tsol_ref,
    brhs,
    trhs,
    blinv,
    buinv,
    tlinv,
    tuinv,
    low,
    up,
    ybuf,
    acc,
    part,
    hubbuf,
    diff,
    ucon,
    ubuf,
    mine,
    cpl,
    bw_ref,
    tw_ref,
    pat_ref,
    par_ref,
    in_sem,
    pair_s,
    pair_r,
    xs_sem,
    xr_sem,
    hub_s,
    hub_r,
    out_s,
    out_r,
    us_s,
    us_r,
    late_sem,
):
    row = lax.axis_index("row")
    col = lax.axis_index("col")
    leaf = lax.axis_index("leaf")
    z, y = lax.div(col, SIDE), lax.rem(col, SIDE)
    late = row == LATE
    is_hub = z == 0

    def remote(src, dst, send_sem, recv_sem, device):
        return pltpu.make_async_remote_copy(
            src_ref=src,
            dst_ref=dst,
            send_sem=send_sem,
            recv_sem=recv_sem,
            device_id=device,
            device_id_type=MESH,
        )

    def load(i, src, dst):
        copy = pltpu.make_async_copy(src, dst, in_sem.at[i])
        copy.start()
        return copy

    barrier = pltpu.get_barrier_semaphore()

    def hello(device):
        pl.semaphore_signal(barrier, inc=1, device_id=device, device_id_type=MESH)

    def masked(value, mask):
        return jnp.where(mask, value, jnp.zeros_like(value))

    def dot(a, b):
        return jnp.dot(a, b, preferred_element_type=F32)

    places = lax.broadcasted_iota(jnp.int32, (W, NRHS), 0)

    def along(dx, to_leaf):
        return (lax.rem(row + dx, NCB), col, to_leaf)

    def own_y(ld_bw, ld_brhs, ld_blinv):
        ld_bw.wait()
        ld_brhs.wait()
        ld_blinv.wait()
        bmask = places < bw_ref[0]
        rhs = masked(brhs[...].astype(F32), bmask).astype(BF16)
        return bmask, masked(dot(blinv[...], rhs), bmask).astype(BF16)

    def couples(layer, ld_pat, ld_par):
        ld_pat.wait()
        ld_par.wait()
        for t in range(TPR):
            for j in range(NCB):
                on = (pat_ref[t, 0, 0, j] > 0) | (par_ref[0, 0, j] == row * TPR + t)
                cpl[layer, pl.ds(t * NCB + j, 1), :] = jnp.full(
                    (1, NRHS), jnp.where(on, 1.0, 0.0), F32
                )

    def finish(layer, bmask, own, ld_buinv):
        usum = jnp.zeros((W, NRHS), F32)
        for s in ROWS:

            @pl.when(s != row)
            def _():
                remote(
                    ubuf.at[s], ubuf.at[s], us_s.at[0, 0], us_r.at[s], along(1, layer)
                ).wait_recv()

            usum += jnp.where(s == row, own, ubuf[s].astype(F32))
        ld_buinv.wait()
        bdiff = masked(ybuf[layer, row].astype(F32) - usum, bmask).astype(BF16)
        bsol_ref[0] = masked(dot(buinv[...], bdiff), bmask)

    @pl.when(leaf == 0)
    def _():
        pair = (row, col, 1)
        ld_blinv = load(0, blinv_h.at[0], blinv)
        ld_brhs = load(1, brhs_h.at[0], brhs)
        ld_bw = load(2, bw_h, bw_ref)
        ld_pat = load(3, pat_h, pat_ref)
        ld_par = load(4, par_h, par_ref)
        ld_buinv = load(5, buinv_h.at[0], buinv)
        bmask, value = own_y(ld_bw, ld_brhs, ld_blinv)
        ybuf[0, row] = value
        couples(0, ld_pat, ld_par)
        pl.semaphore_wait(barrier, 1)
        sends = [
            remote(ybuf.at[0, row], ybuf.at[0, row], pair_s.at[0], pair_r.at[0], pair),
            remote(cpl.at[0], cpl.at[0], pair_s.at[1], pair_r.at[1], pair),
            remote(low_h.at[:, 0, 0], low.at[0], pair_s.at[2], pair_r.at[2], pair),
            remote(up_h.at[:, 0, 0], up.at[0], pair_s.at[3], pair_r.at[3], pair),
        ]
        for send in sends:
            send.start()
        for send in sends:
            send.wait_send()
        remote(mine, mine, pair_s.at[4], pair_r.at[4], pair).wait_recv()
        finish(0, bmask, mine[...], ld_buinv)
        remote(tsol_ref, tsol_ref, pair_s.at[5], pair_r.at[5], pair).wait_recv()

    def to_hub(h):
        rows = chunk_rows(h)
        return remote(
            part.at[rows], hubbuf.at[col], hub_s.at[h], hub_r.at[col], (row, h, 1)
        )

    def hand(k, to_z, to_y):
        rows = chunk_rows(k)
        return remote(
            diff.at[rows],
            diff.at[rows],
            out_s.at[to_z * SIDE + to_y],
            out_r.at[k],
            (row, to_z * SIDE + to_y, 1),
        )

    @pl.when(leaf == 1)
    def _():
        pair = (row, col, 0)
        hubs = jnp.where(is_hub, HUBS - 1, HUBS)
        hello(pair)

        @pl.when(is_hub)
        def _():
            def greet(c, carry):
                @pl.when(c != col)
                def _():
                    hello((row, c, 1))

                return carry

            lax.fori_loop(0, PLANE, greet, 0)

        @pl.when(late)
        def _():
            pl.semaphore_wait(barrier, hubs + NCB - 1)
            for dx in (2, 1, 3):
                pl.semaphore_signal(
                    late_sem, inc=1, device_id=along(dx, 1), device_id_type=MESH
                )

        @pl.when(jnp.logical_not(late))
        def _():
            for dx in (2, 1, 3):
                hello(along(dx, 1))

        ld_brhs = load(1, brhs_h.at[0], brhs)
        ld_blinv = load(0, blinv_h.at[0], blinv)
        ld_bw = load(2, bw_h, bw_ref)
        ld_low = load(6, low_h.at[:, 0, 0], low.at[1])
        ld_pat = load(3, pat_h, pat_ref)
        ld_par = load(4, par_h, par_ref)
        ld_tw = load(7, tw_h, tw_ref)
        ld_trhs = load(8, trhs_h, trhs)
        ld_tlinv = load(9, tlinv_h, tlinv)
        ld_tuinv = load(10, tuinv_h, tuinv)
        ld_up = load(11, up_h.at[:, 0, 0], up.at[1])
        ld_buinv = load(5, buinv_h.at[0], buinv)

        bmask, value = own_y(ld_bw, ld_brhs, ld_blinv)
        ybuf[1, row] = value

        @pl.when(jnp.logical_not(late))
        def _():
            pl.semaphore_wait(barrier, hubs + NCB - 2)

        def send_y(layer, to):
            return remote(
                ybuf.at[layer, row],
                ybuf.at[layer, row],
                xs_sem.at[layer, to],
                xr_sem.at[layer, row],
                (to, col, 1),
            )

        def wait_y0():
            remote(
                ybuf.at[0, row], ybuf.at[0, row], pair_s.at[0], pair_r.at[0], pair
            ).wait_recv()

        def arrived(layer, s):
            return remote(
                ybuf.at[layer, s],
                ybuf.at[layer, s],
                xs_sem.at[layer, s],
                xr_sem.at[layer, s],
                (s, col, 1),
            )

        for layer in (1, 0):
            if layer == 0:
                wait_y0()
            for dx in (2, 1, 3):
                to = lax.rem(row + dx, NCB)

                @pl.when(late | (to != LATE))
                def _():
                    send_y(layer, to).start()

        @pl.when(jnp.logical_not(late))
        def _():
            pl.semaphore_wait(late_sem, 1)
            for layer in (1, 0):
                send_y(layer, LATE).start()

        couples(1, ld_pat, ld_par)
        ld_low.wait()
        remote(cpl.at[0], cpl.at[0], pair_s.at[1], pair_r.at[1], pair).wait_recv()
        remote(
            low_h.at[:, 0, 0], low.at[0], pair_s.at[2], pair_r.at[2], pair
        ).wait_recv()

        def factor(layer, t, j):
            return cpl[layer, pl.ds(t * NCB + j, 1), :]

        order = (
            row,
            jnp.where(lax.rem(row, 2) == 0, 1, 0),
            jnp.where(row == NCB - 1, 1, NCB - 1),
            jnp.where(late, 0, LATE),
        )
        steps = [(layer, i) for i in range(NCB) for layer in (1, 0)]
        for step, (layer, i) in enumerate(steps):
            s = order[i]
            if i:
                arrived(layer, s).wait_recv()
            vec = ybuf[layer, s]
            if step < len(steps) - 1:
                for t in range(TPR):
                    term = dot(low[layer, t, s], vec) * factor(layer, t, s)
                    rows = pl.ds(t * W, W)
                    if step == 0:
                        acc[rows, :] = term
                    else:
                        acc[rows, :] += term
                continue
            for h in HUB_ORDER:
                t, first = divmod(chunk_of(h) * CH, W)
                term = dot(low[layer, t, s, pl.ds(first, CH), :], vec)
                term *= factor(layer, t, s)
                rows = chunk_rows(h)
                part[rows, :] = (acc[rows, :] + term).astype(BF16)

                @pl.when(col != h)
                def _():
                    to_hub(h).start()

        @pl.when(is_hub)
        def _():
            own = chunk_rows(y)
            hubbuf[col] = part[own, :]

            def add(c, total):
                @pl.when(c != col)
                def _():
                    remote(
                        part.at[own], hubbuf.at[c], hub_s.at[0], hub_r.at[c], (row, c, 1)
                    ).wait_recv()

                return total + hubbuf[c].astype(F32)

            lsum = lax.fori_loop(0, PLANE, add, jnp.zeros((CH, NRHS), F32))
            ld_tw.wait()
            ld_trhs.wait()
            top = lax.div(chunk_of(y), HUBS // TPR)
            first = lax.rem(chunk_of(y), HUBS // TPR) * CH
            here = lax.broadcasted_iota(jnp.int32, (CH, NRHS), 0) + first
            width = jnp.where(top == 0, tw_ref[0], tw_ref[1])
            rest = trhs[top, pl.ds(pl.multiple_of(first, CH), CH), :].astype(F32) - lsum
            diff[own, :] = masked(rest, here < width).astype(BF16)

        @pl.when(jnp.logical_not(is_hub))
        def _():
            ld_tw.wait()
            ld_trhs.wait()
            hand(y, 0, y).wait_recv()

        def to_lines(do, first, last):
            @pl.when(is_hub)
            def _():
                for to_z in range(first, last):
                    do(hand(y, to_z, y))

        def to_line(do):
            for to in NEAR_FIRST:

                @pl.when(y != to)
                def _():
                    do(hand(y, z, to))

        to_lines(lambda copy: copy.start(), 1, 2)
        to_line(lambda copy: copy.start())
        to_lines(lambda copy: copy.start(), 2, SIDE)

        ld_tlinv.wait()
        ld_tuinv.wait()
        halves = []
        for t in range(TPR):
            total = None
            for part_of in range(2):
                first = t * HUBS // TPR + part_of * 2
                for k in NEAR_FIRST[first : first + 2]:

                    @pl.when(y != k)
                    def _():
                        hand(k, z, k).wait_recv()

                rows = pl.ds(first * CH, 2 * CH)
                inner = pl.ds(part_of * 2 * CH, 2 * CH)
                term = dot(tlinv[t, :, inner], diff[rows, :])
                total = term if total is None else total + term
            tmask = places < tw_ref[t]
            top_y = masked(total, tmask).astype(BF16)
            top = masked(dot(tuinv[t], top_y), tmask)
            tsol_ref[t] = top
            halves.append(top.astype(BF16))

        ld_up.wait()
        remote(up_h.at[:, 0, 0], up.at[0], pair_s.at[3], pair_r.at[3], pair).wait_recv()

        def contribution(layer, j):
            total = dot(up[layer, 0, j], halves[0]) * factor(layer, 0, j)
            return total + dot(up[layer, 1, j], halves[1]) * factor(layer, 1, j)

        sends = []
        for layer, dx in ((1, 2), (1, 1), (1, 3), (0, 2), (0, 1), (0, 3)):
            j = lax.rem(row + dx, NCB)
            ucon[layer, dx] = contribution(layer, j).astype(BF16)
            send = remote(
                ucon.at[layer, dx],
                ubuf.at[row],
                us_s.at[layer, dx],
                us_r.at[row],
                (j, col, layer),
            )
            send.start()
            sends.append(send)
        sends.append(remote(tsol_ref, tsol_ref, pair_s.at[5], pair_r.at[5], pair))
        sends[-1].start()
        mine[...] = contribution(0, row)
        sends.append(remote(mine, mine, pair_s.at[4], pair_r.at[4], pair))
        sends[-1].start()
        own = contribution(1, row)

        finish(1, bmask, own, ld_buinv)
        for send in sends:
            send.wait_send()
        for layer in (1, 0):
            for dx in (1, 2, 3):
                to = lax.rem(row + dx, NCB)

                send_y(layer, to).wait_send()
        for h in range(HUBS):

            @pl.when(col != h)
            def _():
                to_hub(h).wait_send()

        to_line(lambda copy: copy.wait_send())
        to_lines(lambda copy: copy.wait_send(), 1, SIDE)


def write(bsol, tsol, bsol_h, tsol_h, sem):
    copies = [
        pltpu.make_async_copy(tsol, tsol_h, sem.at[0]),
        pltpu.make_async_copy(bsol, bsol_h, sem.at[1]),
    ]
    for copy in copies:
        copy.start()
    for copy in copies:
        copy.wait()


def local(*args):
    hbm = pl.BlockSpec(memory_space=pltpu.HBM)
    vmem = pl.BlockSpec(memory_space=pltpu.VMEM)
    dma = pltpu.SemaphoreType.DMA
    solved = pl.pallas_call(
        kernel,
        out_shape=(
            pltpu.VMEM((1, W, NRHS), F32),
            pltpu.VMEM((TPR, W, NRHS), F32),
        ),
        in_specs=[hbm] * 12,
        out_specs=(vmem, vmem),
        scratch_shapes=[
            pltpu.VMEM((W, NRHS), BF16),
            pltpu.VMEM((TPR, W, NRHS), BF16),
            pltpu.VMEM((W, W), BF16),
            pltpu.VMEM((W, W), BF16),
            pltpu.VMEM((TPR, W, W), BF16),
            pltpu.VMEM((TPR, W, W), BF16),
            pltpu.VMEM((2, TPR, NCB, W, W), BF16),
            pltpu.VMEM((2, TPR, NCB, W, W), BF16),
            pltpu.VMEM((2, NCB, W, NRHS), BF16),
            pltpu.VMEM((TPR * W, NRHS), F32),
            pltpu.VMEM((TPR * W, NRHS), BF16),
            pltpu.VMEM((PLANE, CH, NRHS), BF16),
            pltpu.VMEM((TPR * W, NRHS), BF16),
            pltpu.VMEM((2, NCB, W, NRHS), BF16),
            pltpu.VMEM((NCB, W, NRHS), BF16),
            pltpu.VMEM((W, NRHS), F32),
            pltpu.VMEM((2, TPR * NCB, NRHS), F32),
            pltpu.SMEM((1,), jnp.int32),
            pltpu.SMEM((TPR,), jnp.int32),
            pltpu.SMEM((TPR, 1, 1, NCB), jnp.int32),
            pltpu.SMEM((1, 1, NCB), jnp.int32),
            dma((12,)),
            dma((6,)),
            dma((6,)),
            dma((2, NCB)),
            dma((2, NCB)),
            dma((HUBS,)),
            dma((PLANE,)),
            dma((PLANE,)),
            dma((HUBS,)),
            dma((2, NCB)),
            dma((NCB,)),
            pltpu.SemaphoreType.REGULAR,
        ],
        compiler_params=pltpu.CompilerParams(
            collective_id=0, has_side_effects=True, vmem_limit_bytes=60 << 20
        ),
        name="substitution",
    )(*args)
    return pl.pallas_call(
        write,
        out_shape=(
            jax.ShapeDtypeStruct((1, W, NRHS), F32),
            jax.ShapeDtypeStruct((TPR, W, NRHS), F32),
        ),
        in_specs=[pl.BlockSpec(memory_space=pl.ANY)] * 2,
        out_specs=(hbm, hbm),
        scratch_shapes=[dma((2,))],
        name="write",
    )(*[pltpu.with_memory_space_constraint(v, pltpu.VMEM) for v in solved])


def solution(mesh):
    placed = (
        P(("row", "col", "leaf"), None, None),
        P("row", None, None),
        P(("row", "col", "leaf"), None, None),
        P(("row", "col", "leaf"), None, None),
        P("row", None, None),
        P("row", None, None),
        P("row", "col", "leaf", None, None, None),
        P("row", "col", "leaf", None, None, None),
        P(("row", "col", "leaf")),
        P("row"),
        P("row", "col", "leaf", None),
        P("col", "leaf", None),
    )
    return jax.shard_map(
        local,
        mesh=mesh,
        in_specs=placed,
        out_specs=(P(("row", "col", "leaf"), None, None), P("row", None, None)),
        check_vma=False,
    )
```

```python
import jax
import jax.numpy as jnp
from jax import lax
from jax.experimental import pallas as pl
from jax.experimental.pallas import tpu as pltpu
from jax.sharding import PartitionSpec as P

MESH = pl.DeviceIdType.MESH
F32 = jnp.float32
BF16 = jnp.bfloat16

W = 256
NRHS = 128
TPR = 2
NCB = 4
SIDE = 8
PLANE = SIDE * SIDE
HUBS = SIDE
CH = TPR * W // HUBS

HUB_ORDER = (4, 3, 5, 2, 6, 1, 7, 0)
NEAR_FIRST = (0, 1, 7, 2, 6, 3, 5, 4)


def chunk_of(hub):
    if isinstance(hub, int):
        return NEAR_FIRST.index(hub)
    side = jnp.where(hub <= SIDE // 2, 2 * hub - 1, 2 * (SIDE - hub))
    return jnp.where(hub == 0, 0, side)


def chunk_rows(hub):
    first = chunk_of(hub) * CH
    return pl.ds(first if isinstance(first, int) else pl.multiple_of(first, CH), CH)
ROWS = (1, 3, 0, 2)
LATE = 2


def kernel(
    brhs_h,
    trhs_h,
    blinv_h,
    buinv_h,
    tlinv_h,
    tuinv_h,
    low_h,
    up_h,
    bw_h,
    tw_h,
    pat_h,
    par_h,
    bsol_ref,
    tsol_ref,
    brhs,
    trhs,
    blinv,
    buinv,
    tlinv,
    tuinv,
    low,
    up,
    ybuf,
    acc,
    part,
    hubbuf,
    diff,
    ucon,
    ubuf,
    mine,
    cpl,
    bw_ref,
    tw_ref,
    pat_ref,
    par_ref,
    in_sem,
    pair_s,
    pair_r,
    xs_sem,
    xr_sem,
    hub_s,
    hub_r,
    out_s,
    out_r,
    us_s,
    us_r,
):
    row = lax.axis_index("row")
    col = lax.axis_index("col")
    leaf = lax.axis_index("leaf")
    z, y = lax.div(col, SIDE), lax.rem(col, SIDE)
    late = row == LATE
    is_hub = z == 0

    def remote(src, dst, send_sem, recv_sem, device):
        return pltpu.make_async_remote_copy(
            src_ref=src,
            dst_ref=dst,
            send_sem=send_sem,
            recv_sem=recv_sem,
            device_id=device,
            device_id_type=MESH,
        )

    def load(i, src, dst):
        copy = pltpu.make_async_copy(src, dst, in_sem.at[i])
        copy.start()
        return copy

    barrier = pltpu.get_barrier_semaphore()

    def hello(device):
        pl.semaphore_signal(barrier, inc=1, device_id=device, device_id_type=MESH)

    def masked(value, mask):
        return jnp.where(mask, value, jnp.zeros_like(value))

    def dot(a, b):
        return jnp.dot(a, b, preferred_element_type=F32)

    places = lax.broadcasted_iota(jnp.int32, (W, NRHS), 0)

    def along(dx, to_leaf):
        return (lax.rem(row + dx, NCB), col, to_leaf)

    def own_y(ld_bw, ld_brhs, ld_blinv):
        ld_bw.wait()
        ld_brhs.wait()
        ld_blinv.wait()
        bmask = places < bw_ref[0]
        rhs = masked(brhs[...].astype(F32), bmask).astype(BF16)
        return bmask, masked(dot(blinv[...], rhs), bmask).astype(BF16)

    def couples(layer, ld_pat, ld_par):
        ld_pat.wait()
        ld_par.wait()
        for t in range(TPR):
            for j in range(NCB):
                on = (pat_ref[t, 0, 0, j] > 0) | (par_ref[0, 0, j] == row * TPR + t)
                cpl[layer, pl.ds(t * NCB + j, 1), :] = jnp.full(
                    (1, NRHS), jnp.where(on, 1.0, 0.0), F32
                )

    def finish(layer, bmask, own, ld_buinv):
        usum = jnp.zeros((W, NRHS), F32)
        for s in ROWS:

            @pl.when(s != row)
            def _():
                remote(
                    ubuf.at[s], ubuf.at[s], us_s.at[0, 0], us_r.at[s], along(1, layer)
                ).wait_recv()

            usum += jnp.where(s == row, own, ubuf[s].astype(F32))
        ld_buinv.wait()
        bdiff = masked(ybuf[layer, row].astype(F32) - usum, bmask).astype(BF16)
        bsol_ref[0] = masked(dot(buinv[...], bdiff), bmask)

    @pl.when(leaf == 0)
    def _():
        pair = (row, col, 1)
        ld_blinv = load(0, blinv_h.at[0], blinv)
        ld_brhs = load(1, brhs_h.at[0], brhs)
        ld_bw = load(2, bw_h, bw_ref)
        ld_pat = load(3, pat_h, pat_ref)
        ld_par = load(4, par_h, par_ref)
        ld_buinv = load(5, buinv_h.at[0], buinv)
        bmask, value = own_y(ld_bw, ld_brhs, ld_blinv)
        ybuf[0, row] = value
        pl.semaphore_wait(barrier, 1)
        sends = [
            remote(ybuf.at[0, row], ybuf.at[0, row], pair_s.at[0], pair_r.at[0], pair),
            remote(cpl.at[0], cpl.at[0], pair_s.at[1], pair_r.at[1], pair),
            remote(low_h.at[:, 0, 0], low.at[0], pair_s.at[2], pair_r.at[2], pair),
            remote(up_h.at[:, 0, 0], up.at[0], pair_s.at[3], pair_r.at[3], pair),
        ]
        sends[0].start()
        couples(0, ld_pat, ld_par)
        for send in sends[1:]:
            send.start()
        for send in sends:
            send.wait_send()
        remote(mine, mine, pair_s.at[4], pair_r.at[4], pair).wait_recv()
        finish(0, bmask, mine[...], ld_buinv)
        remote(tsol_ref, tsol_ref, pair_s.at[5], pair_r.at[5], pair).wait_recv()

    def to_hub(h):
        rows = chunk_rows(h)
        return remote(
            part.at[rows], hubbuf.at[col], hub_s.at[h], hub_r.at[col], (row, h, 1)
        )

    def hand(k, to_z, to_y):
        rows = chunk_rows(k)
        return remote(
            diff.at[rows],
            diff.at[rows],
            out_s.at[to_z * SIDE + to_y],
            out_r.at[k],
            (row, to_z * SIDE + to_y, 1),
        )

    @pl.when(leaf == 1)
    def _():
        pair = (row, col, 0)
        hubs = jnp.where(is_hub, HUBS - 1, HUBS)
        hello(pair)

        for dx in (2, 1, 3):
            hello(along(dx, 1))

        ld_brhs = load(1, brhs_h.at[0], brhs)
        ld_blinv = load(0, blinv_h.at[0], blinv)
        ld_bw = load(2, bw_h, bw_ref)

        @pl.when(is_hub)
        def _():
            def greet(c, carry):
                @pl.when(c != col)
                def _():
                    hello((row, c, 1))

                return carry

            lax.fori_loop(0, PLANE, greet, 0)

        bmask, value = own_y(ld_bw, ld_brhs, ld_blinv)
        ybuf[1, row] = value

        pl.semaphore_wait(barrier, hubs + NCB - 1)

        def send_y(layer, to):
            return remote(
                ybuf.at[layer, row],
                ybuf.at[layer, row],
                xs_sem.at[layer, to],
                xr_sem.at[layer, row],
                (to, col, 1),
            )

        def wait_y0():
            remote(
                ybuf.at[0, row], ybuf.at[0, row], pair_s.at[0], pair_r.at[0], pair
            ).wait_recv()

        def arrived(layer, s):
            return remote(
                ybuf.at[layer, s],
                ybuf.at[layer, s],
                xs_sem.at[layer, s],
                xr_sem.at[layer, s],
                (s, col, 1),
            )

        def send_to_others(layer):
            for dx in (2, 1, 3):
                to = lax.rem(row + dx, NCB)

                @pl.when(late | (to != LATE))
                def _():
                    send_y(layer, to).start()

        def send_to_late(layer):
            @pl.when(jnp.logical_not(late))
            def _():
                send_y(layer, LATE).start()

        @pl.when(late)
        def _():
            send_to_others(1)

        send_to_late(1)
        ld_low = load(6, low_h.at[:, 0, 0], low.at[1])
        ld_pat = load(3, pat_h, pat_ref)
        ld_par = load(4, par_h, par_ref)
        ld_tw = load(7, tw_h, tw_ref)
        ld_trhs = load(8, trhs_h, trhs)
        ld_tlinv = load(9, tlinv_h, tlinv)
        ld_tuinv = load(10, tuinv_h, tuinv)
        ld_up = load(11, up_h.at[:, 0, 0], up.at[1])
        ld_buinv = load(5, buinv_h.at[0], buinv)
        wait_y0()
        send_to_late(0)

        @pl.when(jnp.logical_not(late))
        def _():
            send_to_others(1)

        send_to_others(0)

        couples(1, ld_pat, ld_par)
        ld_low.wait()
        remote(cpl.at[0], cpl.at[0], pair_s.at[1], pair_r.at[1], pair).wait_recv()
        remote(
            low_h.at[:, 0, 0], low.at[0], pair_s.at[2], pair_r.at[2], pair
        ).wait_recv()

        def factor(layer, t, j):
            return cpl[layer, pl.ds(t * NCB + j, 1), :]

        order = (
            row,
            jnp.where(lax.rem(row, 2) == 0, 1, 0),
            jnp.where(row == NCB - 1, 1, NCB - 1),
            jnp.where(late, 0, LATE),
        )
        steps = [(layer, i) for i in range(NCB) for layer in (1, 0)]
        for step, (layer, i) in enumerate(steps):
            s = order[i]
            if i:
                arrived(layer, s).wait_recv()
            vec = ybuf[layer, s]
            if step < len(steps) - 1:
                for t in range(TPR):
                    term = dot(low[layer, t, s], vec) * factor(layer, t, s)
                    rows = pl.ds(t * W, W)
                    if step == 0:
                        acc[rows, :] = term
                    else:
                        acc[rows, :] += term
                continue
            for step in HUB_ORDER:
                h = lax.rem(y + step, HUBS)
                t = lax.div(chunk_of(h), HUBS // TPR)
                first = pl.multiple_of(lax.rem(chunk_of(h), HUBS // TPR) * CH, CH)
                term = dot(low[layer, t, s, pl.ds(first, CH), :], vec)
                term *= factor(layer, t, s)
                rows = chunk_rows(h)
                part[rows, :] = (acc[rows, :] + term).astype(BF16)

                @pl.when(col != h)
                def _():
                    to_hub(h).start()

        @pl.when(is_hub)
        def _():
            own = chunk_rows(y)
            hubbuf[col] = part[own, :]

            def add(c, total):
                @pl.when(c != col)
                def _():
                    remote(
                        part.at[own], hubbuf.at[c], hub_s.at[0], hub_r.at[c], (row, c, 1)
                    ).wait_recv()

                return total + hubbuf[c].astype(F32)

            lsum = lax.fori_loop(0, PLANE, add, jnp.zeros((CH, NRHS), F32))
            ld_tw.wait()
            ld_trhs.wait()
            top = lax.div(chunk_of(y), HUBS // TPR)
            first = lax.rem(chunk_of(y), HUBS // TPR) * CH
            here = lax.broadcasted_iota(jnp.int32, (CH, NRHS), 0) + first
            width = jnp.where(top == 0, tw_ref[0], tw_ref[1])
            rest = trhs[top, pl.ds(pl.multiple_of(first, CH), CH), :].astype(F32) - lsum
            diff[own, :] = masked(rest, here < width).astype(BF16)

        @pl.when(jnp.logical_not(is_hub))
        def _():
            ld_tw.wait()
            ld_trhs.wait()
            hand(y, 0, y).wait_recv()

        def to_lines(do, first, last):
            @pl.when(is_hub)
            def _():
                for to_z in range(first, last):
                    do(hand(y, to_z, y))

        def to_line(do):
            for to in NEAR_FIRST:

                @pl.when(y != to)
                def _():
                    do(hand(y, z, to))

        to_lines(lambda copy: copy.start(), 1, 2)
        to_line(lambda copy: copy.start())
        to_lines(lambda copy: copy.start(), 2, SIDE)

        ld_tlinv.wait()
        ld_tuinv.wait()
        halves = []
        for t in range(TPR):
            total = None
            for part_of in range(2):
                first = t * HUBS // TPR + part_of * 2
                for k in NEAR_FIRST[first : first + 2]:

                    @pl.when(y != k)
                    def _():
                        hand(k, z, k).wait_recv()

                rows = pl.ds(first * CH, 2 * CH)
                inner = pl.ds(part_of * 2 * CH, 2 * CH)
                term = dot(tlinv[t, :, inner], diff[rows, :])
                total = term if total is None else total + term
            tmask = places < tw_ref[t]
            top_y = masked(total, tmask).astype(BF16)
            top = masked(dot(tuinv[t], top_y), tmask)
            tsol_ref[t] = top
            halves.append(top.astype(BF16))

        ld_up.wait()
        remote(up_h.at[:, 0, 0], up.at[0], pair_s.at[3], pair_r.at[3], pair).wait_recv()

        def contribution(layer, j):
            total = dot(up[layer, 0, j], halves[0]) * factor(layer, 0, j)
            return total + dot(up[layer, 1, j], halves[1]) * factor(layer, 1, j)

        sends = []
        for layer, dx in ((1, 2), (1, 3), (1, 1), (0, 2), (0, 3), (0, 1)):
            j = lax.rem(row + dx, NCB)
            ucon[layer, dx] = contribution(layer, j).astype(BF16)
            send = remote(
                ucon.at[layer, dx],
                ubuf.at[row],
                us_s.at[layer, dx],
                us_r.at[row],
                (j, col, layer),
            )
            send.start()
            sends.append(send)
        sends.append(remote(tsol_ref, tsol_ref, pair_s.at[5], pair_r.at[5], pair))
        sends[-1].start()
        mine[...] = contribution(0, row)
        sends.append(remote(mine, mine, pair_s.at[4], pair_r.at[4], pair))
        sends[-1].start()
        own = contribution(1, row)

        for layer in (1, 0):
            for dx in (1, 2, 3):
                to = lax.rem(row + dx, NCB)

                send_y(layer, to).wait_send()
        for h in range(HUBS):

            @pl.when(col != h)
            def _():
                to_hub(h).wait_send()

        to_line(lambda copy: copy.wait_send())
        to_lines(lambda copy: copy.wait_send(), 1, SIDE)

        finish(1, bmask, own, ld_buinv)
        for send in sends:
            send.wait_send()


def write(bsol, tsol, bsol_h, tsol_h, sem):
    copies = [
        pltpu.make_async_copy(tsol, tsol_h, sem.at[0]),
        pltpu.make_async_copy(bsol, bsol_h, sem.at[1]),
    ]
    for copy in copies:
        copy.start()
    for copy in copies:
        copy.wait()


def local(*args):
    hbm = pl.BlockSpec(memory_space=pltpu.HBM)
    vmem = pl.BlockSpec(memory_space=pltpu.VMEM)
    dma = pltpu.SemaphoreType.DMA
    solved = pl.pallas_call(
        kernel,
        out_shape=(
            pltpu.VMEM((1, W, NRHS), F32),
            pltpu.VMEM((TPR, W, NRHS), F32),
        ),
        in_specs=[hbm] * 12,
        out_specs=(vmem, vmem),
        scratch_shapes=[
            pltpu.VMEM((W, NRHS), BF16),
            pltpu.VMEM((TPR, W, NRHS), BF16),
            pltpu.VMEM((W, W), BF16),
            pltpu.VMEM((W, W), BF16),
            pltpu.VMEM((TPR, W, W), BF16),
            pltpu.VMEM((TPR, W, W), BF16),
            pltpu.VMEM((2, TPR, NCB, W, W), BF16),
            pltpu.VMEM((2, TPR, NCB, W, W), BF16),
            pltpu.VMEM((2, NCB, W, NRHS), BF16),
            pltpu.VMEM((TPR * W, NRHS), F32),
            pltpu.VMEM((TPR * W, NRHS), BF16),
            pltpu.VMEM((PLANE, CH, NRHS), BF16),
            pltpu.VMEM((TPR * W, NRHS), BF16),
            pltpu.VMEM((2, NCB, W, NRHS), BF16),
            pltpu.VMEM((NCB, W, NRHS), BF16),
            pltpu.VMEM((W, NRHS), F32),
            pltpu.VMEM((2, TPR * NCB, NRHS), F32),
            pltpu.SMEM((1,), jnp.int32),
            pltpu.SMEM((TPR,), jnp.int32),
            pltpu.SMEM((TPR, 1, 1, NCB), jnp.int32),
            pltpu.SMEM((1, 1, NCB), jnp.int32),
            dma((12,)),
            dma((6,)),
            dma((6,)),
            dma((2, NCB)),
            dma((2, NCB)),
            dma((HUBS,)),
            dma((PLANE,)),
            dma((PLANE,)),
            dma((HUBS,)),
            dma((2, NCB)),
            dma((NCB,)),
        ],
        compiler_params=pltpu.CompilerParams(
            collective_id=0, has_side_effects=True, vmem_limit_bytes=56 << 20
        ),
        name="substitution",
    )(*args)
    return pl.pallas_call(
        write,
        out_shape=(
            jax.ShapeDtypeStruct((1, W, NRHS), F32),
            jax.ShapeDtypeStruct((TPR, W, NRHS), F32),
        ),
        in_specs=[pl.BlockSpec(memory_space=pl.ANY)] * 2,
        out_specs=(hbm, hbm),
        scratch_shapes=[dma((2,))],
        name="write",
    )(*[pltpu.with_memory_space_constraint(v, pltpu.VMEM) for v in solved])


def solution(mesh):
    placed = (
        P(("row", "col", "leaf"), None, None),
        P("row", None, None),
        P(("row", "col", "leaf"), None, None),
        P(("row", "col", "leaf"), None, None),
        P("row", None, None),
        P("row", None, None),
        P("row", "col", "leaf", None, None, None),
        P("row", "col", "leaf", None, None, None),
        P(("row", "col", "leaf")),
        P("row"),
        P("row", "col", "leaf", None),
        P("col", "leaf", None),
    )
    return jax.shard_map(
        local,
        mesh=mesh,
        in_specs=placed,
        out_specs=(P(("row", "col", "leaf"), None, None), P("row", None, None)),
        check_vma=False,
    )
```

```python
import jax
import jax.numpy as jnp
from jax import lax
from jax.experimental import pallas as pl
from jax.experimental.pallas import tpu as pltpu
from jax.sharding import PartitionSpec as P

MESH = pl.DeviceIdType.MESH
F32 = jnp.float32
BF16 = jnp.bfloat16

W = 256
NRHS = 128
TPR = 2
NCB = 4
SIDE = 8
PLANE = SIDE * SIDE
HUBS = SIDE
CH = TPR * W // HUBS

HUB_Z = 1
HUB_ORDER = (4, 3, 5, 2, 6, 1, 7, 0)
NEAR_FIRST = (0, 1, 7, 2, 6, 3, 5, 4)


def chunk_of(hub):
    if isinstance(hub, int):
        return NEAR_FIRST.index(hub)
    side = jnp.where(hub <= SIDE // 2, 2 * hub - 1, 2 * (SIDE - hub))
    return jnp.where(hub == 0, 0, side)


def chunk_rows(hub):
    first = chunk_of(hub) * CH
    return pl.ds(first if isinstance(first, int) else pl.multiple_of(first, CH), CH)
ROWS = (1, 3, 0, 2)
LATE = 2


def kernel(
    brhs_h,
    trhs_h,
    blinv_h,
    buinv_h,
    tlinv_h,
    tuinv_h,
    low_h,
    up_h,
    bw_h,
    tw_h,
    pat_h,
    par_h,
    bsol_ref,
    tsol_ref,
    brhs,
    trhs,
    blinv,
    buinv,
    tlinv,
    tuinv,
    low,
    up,
    ybuf,
    acc,
    part,
    hubbuf,
    diff,
    ucon,
    ubuf,
    mine,
    cpl,
    bw_ref,
    tw_ref,
    pat_ref,
    par_ref,
    in_sem,
    pair_s,
    pair_r,
    xs_sem,
    xr_sem,
    hub_s,
    hub_r,
    out_s,
    out_r,
    us_s,
    us_r,
):
    row = lax.axis_index("row")
    col = lax.axis_index("col")
    leaf = lax.axis_index("leaf")
    z, y = lax.div(col, SIDE), lax.rem(col, SIDE)
    late = row == LATE
    is_hub = z == HUB_Z

    def remote(src, dst, send_sem, recv_sem, device):
        return pltpu.make_async_remote_copy(
            src_ref=src,
            dst_ref=dst,
            send_sem=send_sem,
            recv_sem=recv_sem,
            device_id=device,
            device_id_type=MESH,
        )

    def load(i, src, dst):
        copy = pltpu.make_async_copy(src, dst, in_sem.at[i])
        copy.start()
        return copy

    barrier = pltpu.get_barrier_semaphore()

    def hello(device):
        pl.semaphore_signal(barrier, inc=1, device_id=device, device_id_type=MESH)

    def masked(value, mask):
        return jnp.where(mask, value, jnp.zeros_like(value))

    def dot(a, b):
        return jnp.dot(a, b, preferred_element_type=F32)

    places = lax.broadcasted_iota(jnp.int32, (W, NRHS), 0)

    def along(dx, to_leaf):
        return (lax.rem(row + dx, NCB), col, to_leaf)

    def own_y(ld_bw, ld_brhs, ld_blinv):
        ld_bw.wait()
        ld_brhs.wait()
        ld_blinv.wait()
        bmask = places < bw_ref[0]
        rhs = masked(brhs[...].astype(F32), bmask).astype(BF16)
        return bmask, masked(dot(blinv[...], rhs), bmask).astype(BF16)

    def couples(layer, ld_pat, ld_par):
        ld_pat.wait()
        ld_par.wait()
        for t in range(TPR):
            for j in range(NCB):
                on = (pat_ref[t, 0, 0, j] > 0) | (par_ref[0, 0, j] == row * TPR + t)
                cpl[layer, pl.ds(t * NCB + j, 1), :] = jnp.full(
                    (1, NRHS), jnp.where(on, 1.0, 0.0), F32
                )

    def finish(layer, bmask, own, ld_buinv):
        usum = jnp.zeros((W, NRHS), F32)
        for s in ROWS:

            @pl.when(s != row)
            def _():
                remote(
                    ubuf.at[s], ubuf.at[s], us_s.at[0, 0], us_r.at[s], along(1, layer)
                ).wait_recv()

            usum += jnp.where(s == row, own, ubuf[s].astype(F32))
        ld_buinv.wait()
        bdiff = masked(ybuf[layer, row].astype(F32) - usum, bmask).astype(BF16)
        bsol_ref[0] = masked(dot(buinv[...], bdiff), bmask)

    @pl.when(leaf == 0)
    def _():
        pair = (row, col, 1)
        ld_blinv = load(0, blinv_h.at[0], blinv)
        ld_brhs = load(1, brhs_h.at[0], brhs)
        ld_bw = load(2, bw_h, bw_ref)
        ld_pat = load(3, pat_h, pat_ref)
        ld_par = load(4, par_h, par_ref)
        ld_buinv = load(5, buinv_h.at[0], buinv)
        bmask, value = own_y(ld_bw, ld_brhs, ld_blinv)
        ybuf[0, row] = value
        pl.semaphore_wait(barrier, 1)
        sends = [
            remote(ybuf.at[0, row], ybuf.at[0, row], pair_s.at[0], pair_r.at[0], pair),
            remote(cpl.at[0], cpl.at[0], pair_s.at[1], pair_r.at[1], pair),
            remote(low_h.at[:, 0, 0], low.at[0], pair_s.at[2], pair_r.at[2], pair),
            remote(up_h.at[:, 0, 0], up.at[0], pair_s.at[3], pair_r.at[3], pair),
        ]
        sends[0].start()
        couples(0, ld_pat, ld_par)
        for send in sends[1:]:
            send.start()
        for send in sends:
            send.wait_send()
        remote(mine, mine, pair_s.at[4], pair_r.at[4], pair).wait_recv()
        finish(0, bmask, mine[...], ld_buinv)
        remote(tsol_ref, tsol_ref, pair_s.at[5], pair_r.at[5], pair).wait_recv()

    def to_hub(h):
        rows = chunk_rows(h)
        return remote(
            part.at[rows],
            hubbuf.at[col],
            hub_s.at[h],
            hub_r.at[col],
            (row, HUB_Z * SIDE + h, 1),
        )

    def hand(k, to_z, to_y):
        rows = chunk_rows(k)
        return remote(
            diff.at[rows],
            diff.at[rows],
            out_s.at[to_z * SIDE + to_y],
            out_r.at[k],
            (row, to_z * SIDE + to_y, 1),
        )

    @pl.when(leaf == 1)
    def _():
        pair = (row, col, 0)
        hubs = jnp.where(is_hub, HUBS - 1, HUBS)
        hello(pair)

        for dx in (2, 1, 3):
            hello(along(dx, 1))

        ld_brhs = load(1, brhs_h.at[0], brhs)
        ld_blinv = load(0, blinv_h.at[0], blinv)
        ld_bw = load(2, bw_h, bw_ref)

        @pl.when(is_hub)
        def _():
            def greet(c, carry):
                @pl.when(c != col)
                def _():
                    hello((row, c, 1))

                return carry

            lax.fori_loop(0, PLANE, greet, 0)

        bmask, value = own_y(ld_bw, ld_brhs, ld_blinv)
        ybuf[1, row] = value

        pl.semaphore_wait(barrier, hubs + NCB - 1)

        def send_y(layer, to):
            return remote(
                ybuf.at[layer, row],
                ybuf.at[layer, row],
                xs_sem.at[layer, to],
                xr_sem.at[layer, row],
                (to, col, 1),
            )

        def wait_y0():
            remote(
                ybuf.at[0, row], ybuf.at[0, row], pair_s.at[0], pair_r.at[0], pair
            ).wait_recv()

        def arrived(layer, s):
            return remote(
                ybuf.at[layer, s],
                ybuf.at[layer, s],
                xs_sem.at[layer, s],
                xr_sem.at[layer, s],
                (s, col, 1),
            )

        def send_to_others(layer):
            for dx in (2, 1, 3):
                to = lax.rem(row + dx, NCB)

                @pl.when(late | (to != LATE))
                def _():
                    send_y(layer, to).start()

        def send_to_late(layer):
            @pl.when(jnp.logical_not(late))
            def _():
                send_y(layer, LATE).start()

        @pl.when(late)
        def _():
            send_to_others(1)

        send_to_late(1)
        ld_low = load(6, low_h.at[:, 0, 0], low.at[1])
        ld_pat = load(3, pat_h, pat_ref)
        ld_par = load(4, par_h, par_ref)
        ld_tw = load(7, tw_h, tw_ref)
        ld_trhs = load(8, trhs_h, trhs)
        ld_tlinv = load(9, tlinv_h, tlinv)
        ld_tuinv = load(10, tuinv_h, tuinv)
        ld_up = load(11, up_h.at[:, 0, 0], up.at[1])
        ld_buinv = load(5, buinv_h.at[0], buinv)
        wait_y0()
        send_to_late(0)

        @pl.when(jnp.logical_not(late))
        def _():
            send_to_others(1)

        send_to_others(0)

        couples(1, ld_pat, ld_par)
        ld_low.wait()
        remote(cpl.at[0], cpl.at[0], pair_s.at[1], pair_r.at[1], pair).wait_recv()
        remote(
            low_h.at[:, 0, 0], low.at[0], pair_s.at[2], pair_r.at[2], pair
        ).wait_recv()

        def factor(layer, t, j):
            return cpl[layer, pl.ds(t * NCB + j, 1), :]

        order = (
            row,
            jnp.where(lax.rem(row, 2) == 0, 1, 0),
            jnp.where(row == NCB - 1, 1, NCB - 1),
            jnp.where(late, 0, LATE),
        )
        steps = [(layer, i) for i in range(NCB) for layer in (1, 0)]
        for step, (layer, i) in enumerate(steps):
            s = order[i]
            if i:
                arrived(layer, s).wait_recv()
            vec = ybuf[layer, s]
            if step < len(steps) - 1:
                for t in range(TPR):
                    term = dot(low[layer, t, s], vec) * factor(layer, t, s)
                    rows = pl.ds(t * W, W)
                    if step == 0:
                        acc[rows, :] = term
                    else:
                        acc[rows, :] += term
                continue
            for step in HUB_ORDER:
                h = lax.rem(y + step, HUBS)
                t = lax.div(chunk_of(h), HUBS // TPR)
                first = pl.multiple_of(lax.rem(chunk_of(h), HUBS // TPR) * CH, CH)
                term = dot(low[layer, t, s, pl.ds(first, CH), :], vec)
                term *= factor(layer, t, s)
                rows = chunk_rows(h)
                part[rows, :] = (acc[rows, :] + term).astype(BF16)

                @pl.when(col != HUB_Z * SIDE + h)
                def _():
                    to_hub(h).start()

        @pl.when(is_hub)
        def _():
            own = chunk_rows(y)
            hubbuf[col] = part[own, :]

            def add(c, total):
                @pl.when(c != col)
                def _():
                    remote(
                        part.at[own], hubbuf.at[c], hub_s.at[0], hub_r.at[c], (row, c, 1)
                    ).wait_recv()

                return total + hubbuf[c].astype(F32)

            lsum = lax.fori_loop(0, PLANE, add, jnp.zeros((CH, NRHS), F32))
            ld_tw.wait()
            ld_trhs.wait()
            top = lax.div(chunk_of(y), HUBS // TPR)
            first = lax.rem(chunk_of(y), HUBS // TPR) * CH
            here = lax.broadcasted_iota(jnp.int32, (CH, NRHS), 0) + first
            width = jnp.where(top == 0, tw_ref[0], tw_ref[1])
            rest = trhs[top, pl.ds(pl.multiple_of(first, CH), CH), :].astype(F32) - lsum
            diff[own, :] = masked(rest, here < width).astype(BF16)

        @pl.when(jnp.logical_not(is_hub))
        def _():
            ld_tw.wait()
            ld_trhs.wait()
            hand(y, z, y).wait_recv()

        def to_root_line(do):
            @pl.when(is_hub)
            def _():
                for to in NEAR_FIRST:
                    do(hand(y, 0, to))

        def to_columns(do):
            @pl.when(is_hub)
            def _():
                for to_z in range(HUB_Z + 1, SIDE):
                    do(hand(y, to_z, y))

        def to_line(do):
            for to in NEAR_FIRST:

                @pl.when((y != to) & (z > 0))
                def _():
                    do(hand(y, z, to))

        to_root_line(lambda copy: copy.start())
        to_line(lambda copy: copy.start())
        to_columns(lambda copy: copy.start())

        ld_tlinv.wait()
        ld_tuinv.wait()
        halves = []
        for t in range(TPR):
            total = None
            for part_of in range(2):
                first = t * HUBS // TPR + part_of * 2
                for k in NEAR_FIRST[first : first + 2]:

                    @pl.when(y != k)
                    def _():
                        hand(k, z, k).wait_recv()

                rows = pl.ds(first * CH, 2 * CH)
                inner = pl.ds(part_of * 2 * CH, 2 * CH)
                term = dot(tlinv[t, :, inner], diff[rows, :])
                total = term if total is None else total + term
            tmask = places < tw_ref[t]
            top_y = masked(total, tmask).astype(BF16)
            top = masked(dot(tuinv[t], top_y), tmask)
            tsol_ref[t] = top
            halves.append(top.astype(BF16))

        ld_up.wait()
        remote(up_h.at[:, 0, 0], up.at[0], pair_s.at[3], pair_r.at[3], pair).wait_recv()

        def contribution(layer, j):
            total = dot(up[layer, 0, j], halves[0]) * factor(layer, 0, j)
            return total + dot(up[layer, 1, j], halves[1]) * factor(layer, 1, j)

        sends = []
        for layer, dx in ((1, 2), (1, 3), (1, 1), (0, 2), (0, 3), (0, 1)):
            j = lax.rem(row + dx, NCB)
            ucon[layer, dx] = contribution(layer, j).astype(BF16)
            send = remote(
                ucon.at[layer, dx],
                ubuf.at[row],
                us_s.at[layer, dx],
                us_r.at[row],
                (j, col, layer),
            )
            send.start()
            sends.append(send)
        sends.append(remote(tsol_ref, tsol_ref, pair_s.at[5], pair_r.at[5], pair))
        sends[-1].start()
        mine[...] = contribution(0, row)
        sends.append(remote(mine, mine, pair_s.at[4], pair_r.at[4], pair))
        sends[-1].start()
        own = contribution(1, row)

        for layer in (1, 0):
            for dx in (1, 2, 3):
                to = lax.rem(row + dx, NCB)

                send_y(layer, to).wait_send()
        for h in range(HUBS):

            @pl.when(col != HUB_Z * SIDE + h)
            def _():
                to_hub(h).wait_send()

        to_line(lambda copy: copy.wait_send())
        to_root_line(lambda copy: copy.wait_send())
        to_columns(lambda copy: copy.wait_send())

        finish(1, bmask, own, ld_buinv)
        for send in sends:
            send.wait_send()


def write(bsol, tsol, bsol_h, tsol_h, sem):
    copies = [
        pltpu.make_async_copy(tsol, tsol_h, sem.at[0]),
        pltpu.make_async_copy(bsol, bsol_h, sem.at[1]),
    ]
    for copy in copies:
        copy.start()
    for copy in copies:
        copy.wait()


def local(*args):
    hbm = pl.BlockSpec(memory_space=pltpu.HBM)
    vmem = pl.BlockSpec(memory_space=pltpu.VMEM)
    dma = pltpu.SemaphoreType.DMA
    solved = pl.pallas_call(
        kernel,
        out_shape=(
            pltpu.VMEM((1, W, NRHS), F32),
            pltpu.VMEM((TPR, W, NRHS), F32),
        ),
        in_specs=[hbm] * 12,
        out_specs=(vmem, vmem),
        scratch_shapes=[
            pltpu.VMEM((W, NRHS), BF16),
            pltpu.VMEM((TPR, W, NRHS), BF16),
            pltpu.VMEM((W, W), BF16),
            pltpu.VMEM((W, W), BF16),
            pltpu.VMEM((TPR, W, W), BF16),
            pltpu.VMEM((TPR, W, W), BF16),
            pltpu.VMEM((2, TPR, NCB, W, W), BF16),
            pltpu.VMEM((2, TPR, NCB, W, W), BF16),
            pltpu.VMEM((2, NCB, W, NRHS), BF16),
            pltpu.VMEM((TPR * W, NRHS), F32),
            pltpu.VMEM((TPR * W, NRHS), BF16),
            pltpu.VMEM((PLANE, CH, NRHS), BF16),
            pltpu.VMEM((TPR * W, NRHS), BF16),
            pltpu.VMEM((2, NCB, W, NRHS), BF16),
            pltpu.VMEM((NCB, W, NRHS), BF16),
            pltpu.VMEM((W, NRHS), F32),
            pltpu.VMEM((2, TPR * NCB, NRHS), F32),
            pltpu.SMEM((1,), jnp.int32),
            pltpu.SMEM((TPR,), jnp.int32),
            pltpu.SMEM((TPR, 1, 1, NCB), jnp.int32),
            pltpu.SMEM((1, 1, NCB), jnp.int32),
            dma((12,)),
            dma((6,)),
            dma((6,)),
            dma((2, NCB)),
            dma((2, NCB)),
            dma((HUBS,)),
            dma((PLANE,)),
            dma((PLANE,)),
            dma((HUBS,)),
            dma((2, NCB)),
            dma((NCB,)),
        ],
        compiler_params=pltpu.CompilerParams(
            collective_id=0, has_side_effects=True, vmem_limit_bytes=56 << 20
        ),
        name="substitution",
    )(*args)
    return pl.pallas_call(
        write,
        out_shape=(
            jax.ShapeDtypeStruct((1, W, NRHS), F32),
            jax.ShapeDtypeStruct((TPR, W, NRHS), F32),
        ),
        in_specs=[pl.BlockSpec(memory_space=pl.ANY)] * 2,
        out_specs=(hbm, hbm),
        scratch_shapes=[dma((2,))],
        name="write",
    )(*[pltpu.with_memory_space_constraint(v, pltpu.VMEM) for v in solved])


def solution(mesh):
    placed = (
        P(("row", "col", "leaf"), None, None),
        P("row", None, None),
        P(("row", "col", "leaf"), None, None),
        P(("row", "col", "leaf"), None, None),
        P("row", None, None),
        P("row", None, None),
        P("row", "col", "leaf", None, None, None),
        P("row", "col", "leaf", None, None, None),
        P(("row", "col", "leaf")),
        P("row"),
        P("row", "col", "leaf", None),
        P("col", "leaf", None),
    )
    return jax.shard_map(
        local,
        mesh=mesh,
        in_specs=placed,
        out_specs=(P(("row", "col", "leaf"), None, None), P("row", None, None)),
        check_vma=False,
    )
```
